512 devices in a mesh: grp: 8 (over y, x_lo), feat: 64 (over z, x_hi, core).
Axes of the slice: x: 4 (x_hi: 2, x_lo: 2; x = x_hi * 2 + x_lo), y: 4, z: 16, core: 2. Of those that a mesh axis runs over, the one named last changes fastest.
Arguments:
- grads: float32 [8, 512, 16384], P('grp', None, 'feat'), may hold values from -16 to 16
- partner: int32 [8, 2], replicated, may hold values from 0 to 511, as said below
Outputs:
- self_tile: float32 [8, 512, 512], P('grp', 'feat')
- cross_tile_t: float32 [8, 512, 512], P('grp', 'feat')
The draws below stay inside these ranges and needn't reach their ends.
Inputs may be any that keep to these rules, and one draw needn't show every extreme that they name: partner[g,0] is a group other than g; partner[g,1] is a row offset, different for different groups.
All inputs are finite; a program needn't handle non-finite values.
Results may differ from the reference program's by a relative error of at most 0.0003.
Values sent between devices are 32-bit elements; how exact they have to be, the bound alone decides.
No kernel may reach another device: no remote copies, remote signals or barrier semaphores. Data moves between devices by JAX's collectives and lax.ppermute only.
A program may use at most 64 MiB of HBM per device.

```python
import math
import jax
import jax.numpy as jnp
from jax import lax

K = 16384
ROWS = 512
GROUPS = 8


def draw_partner(key, part):
    key = jax.random.fold_in(key, 7)
    first_key = jax.random.fold_in(key, 1)
    second_key = jax.random.fold_in(key, 2)
    third_key = jax.random.fold_in(key, 3)
    steps = jax.random.randint(first_key, (GROUPS,), 1, GROUPS).astype(jnp.int32)
    groups = (jnp.arange(GROUPS, dtype=jnp.int32) + steps) % GROUPS
    inner = (1 + jax.random.permutation(second_key, ROWS - 2)[:GROUPS - 2]).astype(jnp.int32)
    ends = jnp.array([0, ROWS - 1], dtype=jnp.int32)
    offsets = jax.random.permutation(third_key, jnp.concatenate([ends, inner], axis=0)).astype(jnp.int32)
    return jnp.stack([groups, offsets], axis=1).astype(jnp.int32)


def strengthened(values, own_key, source, target, shards_of, factor):
    def block_of(dim):
        return (jnp.arange(values.shape[dim]) // (values.shape[dim] // shards_of)).reshape((-1,) + (1,) * (values.ndim - 1 - dim))

    first = jax.random.permutation(own_key, shards_of)[block_of(target)]
    other_side = (block_of(target) + shards_of // 2) % shards_of
    return jnp.where((block_of(source) == first) | (block_of(source) == other_side), factor * values, values)


def shard_levels(stream_key, dims, shards, smallest, top_value):
    def one(axis_at, blocks):
        heights = jax.random.uniform(jax.random.fold_in(jax.random.fold_in(stream_key, 6), axis_at), (blocks,), jnp.float32, smallest / len(shards), top_value / len(shards))
        return jnp.repeat(jnp.exp(heights), dims[axis_at] // blocks).reshape((-1,) + (1,) * (len(dims) - axis_at - 1))

    factor_of = one(*shards[0])
    for cut in shards[1:]:
        factor_of = factor_of * one(*cut)
    return factor_of


def noise_with(own_key, extent, width, reach, shards, heavy, kind=jnp.bfloat16):
    entries = width * jax.random.normal(own_key, extent, jnp.float32)
    if shards:
        entries = entries * shard_levels(own_key, extent, shards, -0.22, 0.18)
    return jnp.clip(strengthened(entries, jax.random.fold_in(own_key, 3), *heavy), -reach, reach).astype(kind)


def setup_inputs(seed: int = 0) -> dict:
    streams_of = jax.random.split(jax.random.key(seed), 3)
    grads = noise_with(streams_of[0], (GROUPS, ROWS, K), 1.0, 16.0, ((0, 8), (2, 64)), (2, 1, 64, 4.0), jnp.float32)
    partner = draw_partner(jax.random.fold_in(streams_of[2], 71), 0)
    return {"grads": grads, "partner": partner}


def reference(grads, partner):
    scale = 1.0 / math.sqrt(K)

    def one_group(index):
        own_rows = grads[index]
        whole_mate = grads[partner[index, 0]]
        doubled = jnp.concatenate([whole_mate, whole_mate], axis=0)
        mate_rows = lax.dynamic_slice_in_dim(doubled, partner[index, 1].astype(jnp.int32), ROWS, 0)
        self_part = jnp.dot(own_rows, own_rows.T, preferred_element_type=jnp.float32, precision=lax.Precision.HIGHEST)
        cross_part = jnp.dot(mate_rows, own_rows.T, preferred_element_type=jnp.float32, precision=lax.Precision.HIGHEST)
        return (self_part * scale, cross_part * scale)
    self_tile, cross_tile_t = lax.map(one_group, jnp.arange(GROUPS, dtype=jnp.int32))
    return (self_tile, cross_tile_t)
```

```python
import math

import jax
import jax.numpy as jnp
from jax import lax
from jax.experimental import pallas as pl
from jax.experimental.pallas import tpu as pltpu
from jax.sharding import Mesh, PartitionSpec as P

K = 16384
ROWS = 512
GROUPS = 8
FEATS = 256
Z = 16
QUADS = 4
BAND = 32
RUN = 8
SWAP = [(0, 1), (1, 0)]
NEAR = (0, 2, 1, 3)


def route_kernel(partner_ref, rows_ref, out_ref):
    for g in range(GROUPS):
        mate = partner_ref[g, 0]
        turn = lax.rem(BAND - lax.rem(partner_ref[g, 1], BAND), BAND)
        for v in range(2):
            band = rows_ref[mate, pl.ds(v * BAND, BAND), :]
            band = pltpu.roll(band, turn, 0)
            for q in range(QUADS):
                out_ref[g, q, v] = band[q * RUN : (q + 1) * RUN]


def route(partner, rows):
    return pl.pallas_call(
        route_kernel,
        out_shape=jax.ShapeDtypeStruct((GROUPS, QUADS, 2, RUN, FEATS), jnp.float32),
        in_specs=[pl.BlockSpec(memory_space=pltpu.SMEM), pl.BlockSpec(memory_space=pltpu.VMEM)],
        out_specs=pl.BlockSpec(memory_space=pltpu.VMEM),
        name="route",
    )(partner, rows)


def tiles_kernel(where_ref, own_ref, side_ref, cores_ref, mate_ref, out_ref, left_ref, acc_ref):
    quad = where_ref[0]
    shift = where_ref[1]
    turn = where_ref[2]
    lane_row = lax.broadcasted_iota(jnp.int32, (RUN, FEATS), 0)
    wrapped = lane_row + (turn + quad * RUN) >= BAND
    for i, near in enumerate(NEAR):
        block = (own_ref, side_ref, cores_ref.at[0], cores_ref.at[1])[i]
        source = quad ^ near
        for zo in range(Z):
            start = pl.multiple_of(zo * BAND + quad * RUN, RUN)
            left_ref[pl.ds(zo * RUN, RUN), :] = block[pl.ds(start, RUN), :]
            low = lax.rem(zo + shift, Z)
            high = lax.rem(zo + shift + 1, Z)
            near_rows = mate_ref[low // 2, source, low % 2]
            far_rows = mate_ref[high // 2, source, high % 2]
            left_ref[pl.ds((Z + zo) * RUN, RUN), :] = jnp.where(wrapped, far_rows, near_rows)
        part = lax.dot_general(
            left_ref[...],
            block[...],
            (((1,), (1,)), ((), ())),
            preferred_element_type=jnp.float32,
            precision=lax.Precision.HIGHEST,
        )
        if i == 0:
            acc_ref[...] = part
        elif i < 3:
            acc_ref[...] += part
        else:
            total = acc_ref[...] + part
            for t in range(2):
                for zo in range(Z):
                    at = (t * Z + zo) * RUN
                    out_ref[zo, t] = total[at : at + RUN]


def tiles(where, own, side, cores, mate):
    vmem = pl.BlockSpec(memory_space=pltpu.VMEM)
    return pl.pallas_call(
        tiles_kernel,
        out_shape=jax.ShapeDtypeStruct((Z, 2, RUN, ROWS), jnp.float32),
        in_specs=[pl.BlockSpec(memory_space=pltpu.SMEM), vmem, vmem, vmem, vmem],
        out_specs=vmem,
        scratch_shapes=[
            pltpu.VMEM((2 * Z * RUN, FEATS), jnp.float32),
            pltpu.VMEM((2 * Z * RUN, ROWS), jnp.float32),
        ],
        compiler_params=pltpu.CompilerParams(vmem_limit_bytes=32 << 20),
        name="tiles",
    )(where, own, side, cores, mate)


def local(grads, partner):
    own = grads[0]
    group = lax.axis_index("grp")
    quad = lax.axis_index("xh") * 2 + lax.axis_index("core")
    offset = partner[group, 1]
    where = jnp.stack([quad, offset // BAND, offset % BAND]).astype(jnp.int32)

    side = lax.ppermute(own, "xh", SWAP)
    chunks = lax.all_to_all(own.reshape(GROUPS, ROWS // GROUPS, FEATS), "grp", 0, 0)
    cores = lax.ppermute(jnp.stack([own, side]), "core", SWAP)
    routed = route(partner, chunks)
    mate = lax.all_to_all(
        routed.reshape(GROUPS * QUADS, 2, RUN, FEATS), ("grp", "xh", "core"), 0, 0
    ).reshape(GROUPS, QUADS, 2, RUN, FEATS)
    terms = tiles(where, own, side, cores, mate)
    scale = 1.0 / math.sqrt(K)
    total = jnp.sum(lax.all_to_all(terms, "z", 0, 0), axis=0) * scale
    return total[0][None], total[1][None]


def solution(mesh):
    axes = ("grp", "z", "xh", "core")
    fine = Mesh(mesh.devices.reshape(GROUPS, Z, 2, 2), axes)
    feat = ("z", "xh", "core")
    in_specs = (P("grp", None, feat), P())
    out_specs = (P("grp", feat, None), P("grp", feat, None))
    return jax.shard_map(local, mesh=fine, in_specs=in_specs, out_specs=out_specs, check_vma=False)
```

```python
import math

import jax
import jax.numpy as jnp
from jax import lax
from jax.experimental import pallas as pl
from jax.experimental.pallas import tpu as pltpu
from jax.sharding import Mesh, PartitionSpec as P

K = 16384
ROWS = 512
GROUPS = 8
FEATS = 256
QUAD = 4
BANDS = 8
BAND = 64
RUN = 8
MINE = 128
SWAP = [(0, 1), (1, 0)]
NEAR = (0, 2, 1, 3)
HINT = 5_000_000_000
VMEM = pl.BlockSpec(memory_space=pltpu.VMEM)
SMEM = pl.BlockSpec(memory_space=pltpu.SMEM)


def call(kernel, shape, specs, arrays, limit, flops=0, scratch=()):
    def one(dims):
        return jax.ShapeDtypeStruct(dims, jnp.float32)

    several = isinstance(shape, list)
    return pl.pallas_call(
        kernel,
        out_shape=[one(dims) for dims in shape] if several else one(shape),
        in_specs=specs,
        out_specs=[VMEM] * len(shape) if several else VMEM,
        scratch_shapes=scratch,
        compiler_params=pltpu.CompilerParams(vmem_limit_bytes=limit << 20),
        cost_estimate=pl.CostEstimate(flops=flops, bytes_accessed=0, transcendentals=0),
        name=kernel.__name__,
    )(*arrays)


def run_of(member, xh):
    return member // 2 * 4 + xh * 2 + lax.rem(member, 2)


def route_kernel(partner_ref, rows_ref, out_ref):
    for g in range(GROUPS):
        turn = lax.rem(BAND - lax.rem(partner_ref[g, 1], BAND), BAND)
        band = pltpu.roll(rows_ref[partner_ref[g, 0]], turn, 0)
        for m in range(QUAD):
            for xh in range(2):
                at = (m // 2 * 4 + xh * 2 + m % 2) * RUN
                out_ref[g * QUAD + m, xh] = band[at : at + RUN]


def stack_kernel(own_ref, above_ref, near_ref):
    near_ref[0] = own_ref[...]
    near_ref[1] = above_ref[...]


def halves(values):
    high = values.astype(jnp.bfloat16)
    return high, (values - high.astype(jnp.float32)).astype(jnp.bfloat16)


def dot(left, right):
    return lax.dot_general(left, right, (((1,), (1,)), ((), ())), preferred_element_type=jnp.float32)


def products(blocks, rows_ref, fill):
    total = rest = None
    for i, block in enumerate(blocks):
        fill(i)
        rows_high, rows_low = halves(rows_ref[...])
        high, low = halves(block[...])
        part = dot(high, jnp.concatenate([rows_high, rows_low], axis=0))
        other = dot(low, rows_high)
        total = part if total is None else total + part
        rest = other if rest is None else rest + other
    return (total[:, :MINE] + total[:, MINE:] + rest).T


def blocks_of(near_ref, cores_ref):
    return [near_ref.at[0], near_ref.at[1], cores_ref.at[0], cores_ref.at[1]]


def member():
    return lax.axis_index("zl") * 2 + lax.axis_index("core")


def self_kernel(near_ref, cores_ref, out_ref, rows_ref):
    me = member()
    blocks = blocks_of(near_ref, cores_ref)

    def fill(i):
        for band in range(BANDS):
            for xh in range(2):
                start = pl.multiple_of(band * BAND + run_of(me, xh) * RUN, RUN)
                rows_ref[pl.ds((band * 2 + xh) * RUN, RUN), :] = blocks[i][pl.ds(start, RUN), :]

    out_ref[...] = products(blocks, rows_ref, fill)


def cross_kernel(partner_ref, near_ref, cores_ref, mate_ref, self_ref, out_ref, rows_ref):
    me = member()
    offset = partner_ref[lax.axis_index("grp"), 1]
    shift = offset // BAND
    row = lax.broadcasted_iota(jnp.int32, (RUN, FEATS), 0) + lax.rem(offset, BAND)

    def fill(i):
        source = me ^ NEAR[i]
        for band in range(BANDS):
            low = lax.rem(band + shift, BANDS) * QUAD + source
            high = lax.rem(band + shift + 1, BANDS) * QUAD + source
            for xh in range(2):
                rows_ref[pl.ds((band * 2 + xh) * RUN, RUN), :] = jnp.where(
                    row + run_of(me, xh) * RUN >= BAND, mate_ref[high, xh], mate_ref[low, xh]
                )

    cross = products(blocks_of(near_ref, cores_ref), rows_ref, fill)
    for band in range(BANDS):
        for xh in range(2):
            at = (band * 2 + xh) * RUN
            out_ref[band % 2 * 2 + xh, band // 2, 0] = self_ref[at : at + RUN]
            out_ref[band % 2 * 2 + xh, band // 2, 1] = cross[at : at + RUN]


def middle_kernel(terms_ref, out_ref):
    out_ref[...] = terms_ref[0] + terms_ref[1] + terms_ref[2] + terms_ref[3]


def total_kernel(terms_ref, self_ref, cross_ref):
    total = terms_ref[0]
    for i in range(1, terms_ref.shape[0]):
        total = total + terms_ref[i]
    total = total * (1.0 / math.sqrt(K))
    self_ref[0] = total[0]
    cross_ref[0] = total[1]


def local(grads, partner):
    own = grads[0]
    chunks = lax.all_to_all(own.reshape(GROUPS, BAND, FEATS), "grp", 0, 0)
    above = lax.ppermute(own, "zl", SWAP)
    routed = call(route_kernel, (GROUPS * QUAD, 2, RUN, FEATS), [SMEM, VMEM], (partner, chunks), 8)
    mate = lax.all_to_all(routed, ("grp", "zl", "core"), 0, 0)
    near = call(stack_kernel, (2, ROWS, FEATS), [VMEM, VMEM], (own, above), 8)
    cores = lax.ppermute(near, "core", SWAP)
    scratch = [pltpu.VMEM((MINE, FEATS), jnp.float32)]
    self_rows = call(self_kernel, (MINE, ROWS), [VMEM, VMEM], (near, cores), 12, HINT, scratch)
    terms = call(
        cross_kernel,
        (4, 4, 2, RUN, ROWS),
        [SMEM] + [VMEM] * 4,
        (partner, near, cores, mate, self_rows),
        12,
        0,
        scratch,
    )
    terms = lax.all_to_all(terms, ("zm", "xh"), 0, 0)
    terms = call(middle_kernel, (4, 2, RUN, ROWS), [VMEM], (terms,), 8)
    terms = lax.all_to_all(terms, "zo", 0, 0)
    return tuple(call(total_kernel, [(1, RUN, ROWS)] * 2, [VMEM], (terms,), 8))


def solution(mesh):
    fine = Mesh(mesh.devices.reshape(GROUPS, 4, 2, 2, 2, 2), ("grp", "zo", "zm", "zl", "xh", "core"))
    feat = ("zo", "zm", "zl", "xh", "core")
    in_specs = (P("grp", None, feat), P())
    out_specs = (P("grp", feat, None), P("grp", feat, None))
    return jax.shard_map(local, mesh=fine, in_specs=in_specs, out_specs=out_specs, check_vma=False)
```

```python
import math

import jax
import jax.numpy as jnp
from jax import lax
from jax.experimental import pallas as pl
from jax.experimental.pallas import tpu as pltpu
from jax.sharding import Mesh, PartitionSpec as P

K = 16384
ROWS = 512
GROUPS = 8
FEATS = 256
QUAD = 4
BANDS = 8
BAND = 64
RUN = 8
MINE = 128
SWAP = [(0, 1), (1, 0)]
NEAR = (0, 2, 1, 3)
HINT = 5_000_000_000
VMEM = pl.BlockSpec(memory_space=pltpu.VMEM)
SMEM = pl.BlockSpec(memory_space=pltpu.SMEM)


def call(kernel, shape, specs, arrays, limit, flops=0, scratch=()):
    def one(dims):
        return jax.ShapeDtypeStruct(dims, jnp.float32)

    several = isinstance(shape, list)
    return pl.pallas_call(
        kernel,
        out_shape=[one(dims) for dims in shape] if several else one(shape),
        in_specs=specs,
        out_specs=[VMEM] * len(shape) if several else VMEM,
        scratch_shapes=scratch,
        compiler_params=pltpu.CompilerParams(vmem_limit_bytes=limit << 20),
        cost_estimate=pl.CostEstimate(flops=flops, bytes_accessed=0, transcendentals=0),
        name=kernel.__name__,
    )(*arrays)


def run_of(member, xh):
    return member // 2 * 4 + xh * 2 + lax.rem(member, 2)


def route_kernel(partner_ref, rows_ref, out_ref):
    for g in range(GROUPS):
        turn = lax.rem(BAND - lax.rem(partner_ref[g, 1], BAND), BAND)
        band = pltpu.roll(rows_ref[partner_ref[g, 0]], turn, 0)
        for m in range(QUAD):
            for xh in range(2):
                at = (m // 2 * 4 + xh * 2 + m % 2) * RUN
                out_ref[g * QUAD + m, xh] = band[at : at + RUN]


def stack_kernel(own_ref, above_ref, near_ref):
    near_ref[0] = own_ref[...]
    near_ref[1] = above_ref[...]


def halves(values):
    high = values.astype(jnp.bfloat16)
    return high, (values - high.astype(jnp.float32)).astype(jnp.bfloat16)


def dot(left, right):
    return lax.dot_general(left, right, (((1,), (1,)), ((), ())), preferred_element_type=jnp.float32)


def products(blocks, rows_ref, fill):
    total = rest = None
    for i, block in enumerate(blocks):
        fill(i)
        rows_high, rows_low = halves(rows_ref[...])
        high, low = halves(block[...])
        part = dot(high, jnp.concatenate([rows_high, rows_low], axis=0))
        other = dot(low, rows_high)
        total = part if total is None else total + part
        rest = other if rest is None else rest + other
    return (total[:, :MINE] + total[:, MINE:] + rest).T


def blocks_of(near_ref, cores_ref):
    return [near_ref.at[0], near_ref.at[1], cores_ref.at[0], cores_ref.at[1]]


def member():
    return lax.axis_index("zl") * 2 + lax.axis_index("core")


def self_kernel(near_ref, cores_ref, keep_ref, send_ref, rows_ref):
    me = member()
    xh = lax.axis_index("xh")
    blocks = blocks_of(near_ref, cores_ref)

    def fill(i):
        for part in range(2):
            for band in range(BANDS):
                start = pl.multiple_of(band * BAND + run_of(me, xh ^ part) * RUN, RUN)
                rows_ref[pl.ds((part * BANDS + band) * RUN, RUN), :] = blocks[i][pl.ds(start, RUN), :]

    result = products(blocks, rows_ref, fill)
    for band in range(BANDS):
        keep_ref[band] = result[band * RUN : (band + 1) * RUN]
        send_ref[band] = result[(BANDS + band) * RUN : (BANDS + band + 1) * RUN]


def half_kernel(kept_ref, got_ref, keep_ref, send_ref):
    zm = lax.axis_index("zm")
    for zo in range(4):
        keep_ref[zo] = kept_ref[zo * 2 + zm] + got_ref[zo * 2 + zm]
        send_ref[zo] = kept_ref[zo * 2 + 1 - zm] + got_ref[zo * 2 + 1 - zm]


def cross_kernel(partner_ref, near_ref, cores_ref, mate_ref, out_ref, rows_ref):
    me = member()
    offset = partner_ref[lax.axis_index("grp"), 1]
    shift = offset // BAND
    row = lax.broadcasted_iota(jnp.int32, (RUN, FEATS), 0) + lax.rem(offset, BAND)

    def fill(i):
        source = me ^ NEAR[i]
        for band in range(BANDS):
            low = lax.rem(band + shift, BANDS) * QUAD + source
            high = lax.rem(band + shift + 1, BANDS) * QUAD + source
            for xh in range(2):
                rows_ref[pl.ds((band * 2 + xh) * RUN, RUN), :] = jnp.where(
                    row + run_of(me, xh) * RUN >= BAND, mate_ref[high, xh], mate_ref[low, xh]
                )

    cross = products(blocks_of(near_ref, cores_ref), rows_ref, fill)
    for band in range(BANDS):
        for xh in range(2):
            at = (band * 2 + xh) * RUN
            out_ref[band % 2 * 2 + xh, band // 2] = cross[at : at + RUN]


def middle_kernel(kept_ref, got_ref, cross_ref, out_ref):
    for zo in range(4):
        out_ref[zo, 0] = kept_ref[zo] + got_ref[zo]
        out_ref[zo, 1] = cross_ref[0, zo] + cross_ref[1, zo] + cross_ref[2, zo] + cross_ref[3, zo]


def total_kernel(terms_ref, self_ref, cross_ref):
    total = terms_ref[0]
    for i in range(1, terms_ref.shape[0]):
        total = total + terms_ref[i]
    total = total * (1.0 / math.sqrt(K))
    self_ref[0] = total[0]
    cross_ref[0] = total[1]


def local(grads, partner):
    own = grads[0]
    chunks = lax.all_to_all(own.reshape(GROUPS, BAND, FEATS), "grp", 0, 0)
    above = lax.ppermute(own, "zl", SWAP)
    routed = call(route_kernel, (GROUPS * QUAD, 2, RUN, FEATS), [SMEM, VMEM], (partner, chunks), 8)
    mate = lax.all_to_all(routed, ("grp", "zl", "core"), 0, 0)
    near = call(stack_kernel, (2, ROWS, FEATS), [VMEM, VMEM], (own, above), 8)
    cores = lax.ppermute(near, "core", SWAP)
    scratch = [pltpu.VMEM((MINE, FEATS), jnp.float32)]
    bands, some = (BANDS, RUN, ROWS), (4, RUN, ROWS)
    kept, sent = call(self_kernel, [bands] * 2, [VMEM, VMEM], (near, cores), 12, HINT, scratch)
    kept, sent = call(half_kernel, [some] * 2, [VMEM, VMEM], (kept, lax.ppermute(sent, "xh", SWAP)), 8, 2 * HINT)
    got = lax.ppermute(sent, "zm", SWAP)
    cross = call(
        cross_kernel, (4, 4, RUN, ROWS), [SMEM] + [VMEM] * 3, (partner, near, cores, mate), 12, 0, scratch
    )
    cross = lax.all_to_all(cross, ("zm", "xh"), 0, 0)
    terms = call(middle_kernel, (4, 2, RUN, ROWS), [VMEM] * 3, (kept, got, cross), 8)
    terms = lax.all_to_all(terms, "zo", 0, 0)
    return tuple(call(total_kernel, [(1, RUN, ROWS)] * 2, [VMEM], (terms,), 8))


def solution(mesh):
    fine = Mesh(mesh.devices.reshape(GROUPS, 4, 2, 2, 2, 2), ("grp", "zo", "zm", "zl", "xh", "core"))
    feat = ("zo", "zm", "zl", "xh", "core")
    in_specs = (P("grp", None, feat), P())
    out_specs = (P("grp", feat, None), P("grp", feat, None))
    return jax.shard_map(local, mesh=fine, in_specs=in_specs, out_specs=out_specs, check_vma=False)
```

```python
import math

import jax
import jax.numpy as jnp
from jax import lax
from jax.experimental import pallas as pl
from jax.experimental.pallas import tpu as pltpu
from jax.sharding import Mesh, PartitionSpec as P

K = 16384
ROWS = 512
GROUPS = 8
FEATS = 256
QUAD = 4
BANDS = 8
BAND = 64
RUN = 8
MINE = 128
SWAP = [(0, 1), (1, 0)]
NEAR = (0, 2, 1, 3)
HINT = 5_000_000_000
QUARTERS = (2, 3, 0, 1)
VMEM = pl.BlockSpec(memory_space=pltpu.VMEM)
SMEM = pl.BlockSpec(memory_space=pltpu.SMEM)


def call(kernel, shape, specs, arrays, limit, flops=0, scratch=()):
    def one(dims):
        return jax.ShapeDtypeStruct(dims, jnp.float32)

    several = isinstance(shape, list)
    return pl.pallas_call(
        kernel,
        out_shape=[one(dims) for dims in shape] if several else one(shape),
        in_specs=specs,
        out_specs=[VMEM] * len(shape) if several else VMEM,
        scratch_shapes=scratch,
        compiler_params=pltpu.CompilerParams(vmem_limit_bytes=limit << 20),
        cost_estimate=pl.CostEstimate(flops=flops, bytes_accessed=0, transcendentals=0),
        name=kernel.__name__,
    )(*arrays)


def run_of(member, xh):
    return member // 2 * 4 + xh * 2 + lax.rem(member, 2)


def route_kernel(partner_ref, rows_ref, out_ref):
    for g in range(GROUPS):
        turn = lax.rem(BAND - lax.rem(partner_ref[g, 1], BAND), BAND)
        band = pltpu.roll(rows_ref[partner_ref[g, 0]], turn, 0)
        for m in range(QUAD):
            for xh in range(2):
                at = (m // 2 * 4 + xh * 2 + m % 2) * RUN
                out_ref[g * QUAD + m, xh] = band[at : at + RUN]


def stack_kernel(own_ref, above_ref, near_ref):
    near_ref[0] = own_ref[...]
    near_ref[1] = above_ref[...]


def halves(values):
    high = values.astype(jnp.bfloat16)
    return high, (values - high.astype(jnp.float32)).astype(jnp.bfloat16)


def dot(left, right):
    return lax.dot_general(left, right, (((1,), (1,)), ((), ())), preferred_element_type=jnp.float32)


def products(blocks, rows_ref, fill):
    total = rest = None
    for i, block in enumerate(blocks):
        fill(i)
        rows_high, rows_low = halves(rows_ref[...])
        high, low = halves(block[...])
        part = dot(high, jnp.concatenate([rows_high, rows_low], axis=0))
        other = dot(low, rows_high)
        total = part if total is None else total + part
        rest = other if rest is None else rest + other
    return (total[:, :MINE] + total[:, MINE:] + rest).T


def blocks_of(near_ref, cores_ref):
    return [near_ref.at[0], near_ref.at[1], cores_ref.at[0], cores_ref.at[1]]


def member():
    return lax.axis_index("zl") * 2 + lax.axis_index("core")


def self_kernel(near_ref, cores_ref, keep_ref, send_ref, rows_ref):
    me = member()
    zm = lax.axis_index("zm")
    blocks = blocks_of(near_ref, cores_ref)

    def fill(i):
        for part in range(2):
            for at in range(BANDS):
                band = at // 2 * 2 + (zm ^ part)
                start = pl.multiple_of(band * BAND + run_of(me, at % 2) * RUN, RUN)
                rows_ref[pl.ds((part * BANDS + at) * RUN, RUN), :] = blocks[i][pl.ds(start, RUN), :]

    result = products(blocks, rows_ref, fill)
    for band in range(BANDS):
        keep_ref[band] = result[band * RUN : (band + 1) * RUN]
        send_ref[band] = result[(BANDS + band) * RUN : (BANDS + band + 1) * RUN]


def half_kernel(kept_ref, got_ref, keep_ref, send_ref):
    xh = lax.axis_index("xh")
    for zo in range(4):
        keep_ref[zo] = kept_ref[zo * 2 + xh] + got_ref[zo * 2 + xh]
        send_ref[zo] = kept_ref[zo * 2 + 1 - xh] + got_ref[zo * 2 + 1 - xh]


def cross_kernel(partner_ref, near_ref, cores_ref, mate_ref, out_ref, rows_ref):
    me = member()
    offset = partner_ref[lax.axis_index("grp"), 1]
    shift = offset // BAND
    row = lax.broadcasted_iota(jnp.int32, (RUN, FEATS), 0) + lax.rem(offset, BAND)

    def fill(i):
        source = me ^ NEAR[i]
        for band in range(BANDS):
            low = lax.rem(band + shift, BANDS) * QUAD + source
            high = lax.rem(band + shift + 1, BANDS) * QUAD + source
            for xh in range(2):
                rows_ref[pl.ds((band * 2 + xh) * RUN, RUN), :] = jnp.where(
                    row + run_of(me, xh) * RUN >= BAND, mate_ref[high, xh], mate_ref[low, xh]
                )

    cross = products(blocks_of(near_ref, cores_ref), rows_ref, fill)
    for band in range(BANDS):
        for xh in range(2):
            at = (band * 2 + xh) * RUN
            out_ref[band % 2 * 2 + xh, band // 2] = cross[at : at + RUN]


def middle_kernel(kept_ref, got_ref, cross_ref, out_ref):
    for at, zo in enumerate(QUARTERS):
        out_ref[at, 0] = kept_ref[zo] + got_ref[zo]
        out_ref[at, 1] = cross_ref[0, zo] + cross_ref[1, zo] + cross_ref[2, zo] + cross_ref[3, zo]


def total_kernel(terms_ref, self_ref, cross_ref):
    total = terms_ref[0]
    for i in range(1, terms_ref.shape[0]):
        total = total + terms_ref[i]
    total = total * (1.0 / math.sqrt(K))
    self_ref[0] = total[0]
    cross_ref[0] = total[1]


def local(grads, partner):
    own = grads[0]
    chunks = lax.all_to_all(own.reshape(GROUPS, BAND, FEATS), "grp", 0, 0)
    above = lax.ppermute(own, "zl", SWAP)
    routed = call(route_kernel, (GROUPS * QUAD, 2, RUN, FEATS), [SMEM, VMEM], (partner, chunks), 8)
    mate = lax.all_to_all(routed, ("grp", "zl", "core"), 0, 0)
    near = call(stack_kernel, (2, ROWS, FEATS), [VMEM, VMEM], (own, above), 8)
    cores = lax.ppermute(near, "core", SWAP)
    scratch = [pltpu.VMEM((MINE, FEATS), jnp.float32)]
    bands, some = (BANDS, RUN, ROWS), (4, RUN, ROWS)
    kept, sent = call(self_kernel, [bands] * 2, [VMEM, VMEM], (near, cores), 12, HINT, scratch)
    kept, sent = call(half_kernel, [some] * 2, [VMEM, VMEM], (kept, lax.ppermute(sent, "zm", SWAP)), 8, 2 * HINT)
    got = lax.ppermute(sent, "xh", SWAP)
    cross = call(
        cross_kernel, (4, 4, RUN, ROWS), [SMEM] + [VMEM] * 3, (partner, near, cores, mate), 12, 0, scratch
    )
    cross = lax.all_to_all(cross, ("zm", "xh"), 0, 0)
    terms = call(middle_kernel, (4, 2, RUN, ROWS), [VMEM] * 3, (kept, got, cross), 8)
    terms = lax.all_to_all(terms, "zo", 0, 0, axis_index_groups=[list(QUARTERS)])
    return tuple(call(total_kernel, [(1, RUN, ROWS)] * 2, [VMEM], (terms,), 8))


def solution(mesh):
    fine = Mesh(mesh.devices.reshape(GROUPS, 4, 2, 2, 2, 2), ("grp", "zo", "zm", "zl", "xh", "core"))
    feat = ("zo", "zm", "zl", "xh", "core")
    in_specs = (P("grp", None, feat), P())
    out_specs = (P("grp", feat, None), P("grp", feat, None))
    return jax.shard_map(local, mesh=fine, in_specs=in_specs, out_specs=out_specs, check_vma=False)
```

```python
import math

import jax
import jax.numpy as jnp
from jax import lax
from jax.experimental import pallas as pl
from jax.experimental.pallas import tpu as pltpu
from jax.sharding import Mesh, PartitionSpec as P

K = 16384
ROWS = 512
GROUPS = 8
FEATS = 256
QUAD = 4
BANDS = 8
BAND = 64
RUN = 8
MINE = 128
SWAP = [(0, 1), (1, 0)]
NEAR = (0, 2, 1, 3)
HINT = 5_000_000_000
FIRST, SECOND, NARROW, WIDE = 4, 16, 1, 2
VMEM = pl.BlockSpec(memory_space=pltpu.VMEM)


def exchange(values, axes, first):
    members = [i ^ first for i in range(values.shape[0])]
    return lax.all_to_all(values, axes, 0, 0, axis_index_groups=[members])


def call(kernel, shape, specs, arrays, limit, flops=0, scratch=()):
    def one(dims):
        return jax.ShapeDtypeStruct(dims, jnp.float32)

    several = isinstance(shape, list)
    return pl.pallas_call(
        kernel,
        out_shape=[one(dims) for dims in shape] if several else one(shape),
        in_specs=specs,
        out_specs=[VMEM] * len(shape) if several else VMEM,
        scratch_shapes=scratch,
        compiler_params=pltpu.CompilerParams(vmem_limit_bytes=limit << 20),
        cost_estimate=pl.CostEstimate(flops=flops, bytes_accessed=0, transcendentals=0),
        name=kernel.__name__,
    )(*arrays)


def run_of(member, xh):
    return member // 2 * 4 + xh * 2 + lax.rem(member, 2)


def route_kernel(partner_ref, rows_ref, out_ref):
    partner = partner_ref[...]
    for g in range(GROUPS):
        turn = lax.rem(BAND - lax.rem(partner[g, 1], BAND), BAND)
        band = pltpu.roll(rows_ref[partner[g, 0] ^ FIRST], turn, 0)
        for m in range(QUAD):
            for xh in range(2):
                at = (m // 2 * 4 + xh * 2 + m % 2) * RUN
                out_ref[(g * QUAD + m) ^ SECOND, xh] = band[at : at + RUN]


def stack_kernel(own_ref, above_ref, near_ref):
    near_ref[0] = own_ref[...]
    near_ref[1] = above_ref[...]


def halves(values):
    high = values.astype(jnp.bfloat16)
    return high, (values - high.astype(jnp.float32)).astype(jnp.bfloat16)


def dot(left, right):
    return lax.dot_general(left, right, (((1,), (1,)), ((), ())), preferred_element_type=jnp.float32)


def products(blocks, rows_ref, fill):
    total = rest = None
    for i, block in enumerate(blocks):
        fill(i)
        rows_high, rows_low = halves(rows_ref[...])
        high, low = halves(block[...])
        part = dot(high, jnp.concatenate([rows_high, rows_low], axis=0))
        other = dot(low, rows_high)
        total = part if total is None else total + part
        rest = other if rest is None else rest + other
    return (total[:, :MINE] + total[:, MINE:] + rest).T


def blocks_of(near_ref, cores_ref):
    return [near_ref.at[0], near_ref.at[1], cores_ref.at[0], cores_ref.at[1]]


def member():
    return lax.axis_index("zl") * 2 + lax.axis_index("core")


def self_kernel(near_ref, cores_ref, keep_ref, send_ref, rows_ref):
    me = member()
    zm = lax.axis_index("zm")
    blocks = blocks_of(near_ref, cores_ref)

    def fill(i):
        for part in range(2):
            for at in range(BANDS):
                band = at // 2 * 2 + (zm ^ part)
                start = pl.multiple_of(band * BAND + run_of(me, at % 2) * RUN, RUN)
                rows_ref[pl.ds((part * BANDS + at) * RUN, RUN), :] = blocks[i][pl.ds(start, RUN), :]

    result = products(blocks, rows_ref, fill)
    for band in range(BANDS):
        keep_ref[band] = result[band * RUN : (band + 1) * RUN]
        send_ref[band] = result[(BANDS + band) * RUN : (BANDS + band + 1) * RUN]


def half_kernel(kept_ref, got_ref, keep_ref, send_ref):
    xh = lax.axis_index("xh")
    for zo in range(4):
        keep_ref[zo] = kept_ref[zo * 2 + xh] + got_ref[zo * 2 + xh]
        send_ref[zo] = kept_ref[zo * 2 + 1 - xh] + got_ref[zo * 2 + 1 - xh]


def cross_kernel(partner_ref, near_ref, cores_ref, mate_ref, out_ref, rows_ref):
    me = member()
    offset = partner_ref[pl.ds(lax.axis_index("grp"), 1), :][0, 1]
    shift = offset // BAND
    row = lax.broadcasted_iota(jnp.int32, (RUN, FEATS), 0) + lax.rem(offset, BAND)

    def fill(i):
        source = me ^ NEAR[i]
        for band in range(BANDS):
            low = ((lax.rem(band + shift, BANDS) ^ FIRST) * QUAD + source) ^ SECOND
            high = ((lax.rem(band + shift + 1, BANDS) ^ FIRST) * QUAD + source) ^ SECOND
            for xh in range(2):
                rows_ref[pl.ds((band * 2 + xh) * RUN, RUN), :] = jnp.where(
                    row + run_of(me, xh) * RUN >= BAND, mate_ref[high, xh], mate_ref[low, xh]
                )

    cross = products(blocks_of(near_ref, cores_ref), rows_ref, fill)
    for band in range(BANDS):
        for xh in range(2):
            at = (band * 2 + xh) * RUN
            out_ref[(band % 2 * 2 + xh) ^ NARROW, band // 2] = cross[at : at + RUN]


def middle_kernel(kept_ref, got_ref, cross_ref, out_ref):
    for zo in range(4):
        out_ref[zo ^ WIDE, 0] = kept_ref[zo] + got_ref[zo]
        out_ref[zo ^ WIDE, 1] = cross_ref[0, zo] + cross_ref[1, zo] + cross_ref[2, zo] + cross_ref[3, zo]


def total_kernel(terms_ref, self_ref, cross_ref):
    total = terms_ref[0]
    for i in range(1, terms_ref.shape[0]):
        total = total + terms_ref[i]
    total = total * (1.0 / math.sqrt(K))
    self_ref[0] = total[0]
    cross_ref[0] = total[1]


def local(grads, partner):
    own = grads[0]
    chunks = exchange(own.reshape(GROUPS, BAND, FEATS), "grp", FIRST)
    above = lax.ppermute(own, "zl", SWAP)
    routed = call(route_kernel, (GROUPS * QUAD, 2, RUN, FEATS), [VMEM, VMEM], (partner, chunks), 8)
    mate = exchange(routed, ("grp", "zl", "core"), SECOND)
    near = call(stack_kernel, (2, ROWS, FEATS), [VMEM, VMEM], (own, above), 8)
    cores = lax.ppermute(near, "core", SWAP)
    scratch = [pltpu.VMEM((MINE, FEATS), jnp.float32)]
    bands, some = (BANDS, RUN, ROWS), (4, RUN, ROWS)
    kept, sent = call(self_kernel, [bands] * 2, [VMEM, VMEM], (near, cores), 12, HINT, scratch)
    kept, sent = call(half_kernel, [some] * 2, [VMEM, VMEM], (kept, lax.ppermute(sent, "zm", SWAP)), 8, 2 * HINT)
    got = lax.ppermute(sent, "xh", SWAP)
    cross = call(
        cross_kernel, (4, 4, RUN, ROWS), [VMEM] * 4, (partner, near, cores, mate), 12, 0, scratch
    )
    cross = exchange(cross, ("zm", "xh"), NARROW)
    terms = call(middle_kernel, (4, 2, RUN, ROWS), [VMEM] * 3, (kept, got, cross), 8)
    terms = exchange(terms, "zo", WIDE)
    return tuple(call(total_kernel, [(1, RUN, ROWS)] * 2, [VMEM], (terms,), 8))


def solution(mesh):
    fine = Mesh(mesh.devices.reshape(GROUPS, 4, 2, 2, 2, 2), ("grp", "zo", "zm", "zl", "xh", "core"))
    feat = ("zo", "zm", "zl", "xh", "core")
    in_specs = (P("grp", None, feat), P())
    out_specs = (P("grp", feat, None), P("grp", feat, None))
    return jax.shard_map(local, mesh=fine, in_specs=in_specs, out_specs=out_specs, check_vma=False)
```

```python
import math

import jax
import jax.numpy as jnp
from jax import lax
from jax.experimental import pallas as pl
from jax.experimental.pallas import tpu as pltpu
from jax.sharding import Mesh, PartitionSpec as P

K = 16384
ROWS = 512
GROUPS = 8
FEATS = 256
QUAD = 4
BANDS = 8
BAND = 64
RUN = 8
MINE = 128
SWAP = [(0, 1), (1, 0)]
NEAR = (0, 2, 1, 3)
HINT = 5_000_000_000
FIRST, SECOND, NARROW, WIDE = 4, 16, 1, 2
VMEM = pl.BlockSpec(memory_space=pltpu.VMEM)


def exchange(values, axes, first):
    members = [i ^ first for i in range(values.shape[0])]
    return lax.all_to_all(values, axes, 0, 0, axis_index_groups=[members])


def call(kernel, shape, specs, arrays, limit, flops=0, scratch=()):
    def one(dims):
        return dims if isinstance(dims, jax.ShapeDtypeStruct) else jax.ShapeDtypeStruct(dims, jnp.float32)

    several = isinstance(shape, list)
    return pl.pallas_call(
        kernel,
        out_shape=[one(dims) for dims in shape] if several else one(shape),
        in_specs=specs,
        out_specs=[VMEM] * len(shape) if several else VMEM,
        scratch_shapes=scratch,
        compiler_params=pltpu.CompilerParams(vmem_limit_bytes=limit << 20),
        cost_estimate=pl.CostEstimate(flops=flops, bytes_accessed=0, transcendentals=0),
        name=kernel.__name__,
    )(*arrays)


def run_of(member, xh):
    return member // 2 * 4 + xh * 2 + lax.rem(member, 2)


def route_kernel(partner_ref, rows_ref, out_ref):
    partner = partner_ref[...]
    for g in range(GROUPS):
        turn = lax.rem(BAND - lax.rem(partner[g, 1], BAND), BAND)
        band = pltpu.roll(rows_ref[partner[g, 0] ^ FIRST], turn, 0)
        for m in range(QUAD):
            for xh in range(2):
                at = (m // 2 * 4 + xh * 2 + m % 2) * RUN
                out_ref[(g * QUAD + m) ^ SECOND, xh] = band[at : at + RUN]


def stack_kernel(own_ref, above_ref, near_ref):
    near_ref[0] = own_ref[...]
    near_ref[1] = above_ref[...]


def halves(values):
    high = values.astype(jnp.bfloat16)
    return high, (values - high.astype(jnp.float32)).astype(jnp.bfloat16)


def dot(left, right):
    return lax.dot_general(left, right, (((1,), (1,)), ((), ())), preferred_element_type=jnp.float32)


def products(high_ref, low_ref, rows_ref):
    rows_high, rows_low = halves(rows_ref[...])
    part = dot(high_ref[...], jnp.concatenate([rows_high, rows_low], axis=0))
    return (part[:, :MINE] + part[:, MINE:] + dot(low_ref[...], rows_high)).T


def columns(i):
    return pl.ds(i * FEATS, FEATS)


def blocks_of(near_ref, cores_ref):
    return [near_ref.at[0], near_ref.at[1], cores_ref.at[0], cores_ref.at[1]]


def member():
    return lax.axis_index("zl") * 2 + lax.axis_index("core")


def self_kernel(near_ref, cores_ref, keep_ref, send_ref, high_ref, low_ref, rows_ref):
    me = member()
    zm = lax.axis_index("zm")
    blocks = blocks_of(near_ref, cores_ref)

    for i in range(QUAD):
        high_ref[:, columns(i)], low_ref[:, columns(i)] = halves(blocks[i][...])
        for part in range(2):
            for at in range(BANDS):
                band = at // 2 * 2 + (zm ^ part)
                start = pl.multiple_of(band * BAND + run_of(me, at % 2) * RUN, RUN)
                rows_ref[pl.ds((part * BANDS + at) * RUN, RUN), columns(i)] = blocks[i][pl.ds(start, RUN), :]

    result = products(high_ref, low_ref, rows_ref)
    for band in range(BANDS):
        keep_ref[band] = result[band * RUN : (band + 1) * RUN]
        send_ref[band] = result[(BANDS + band) * RUN : (BANDS + band + 1) * RUN]


def half_kernel(kept_ref, got_ref, keep_ref, send_ref):
    xh = lax.axis_index("xh")
    for zo in range(4):
        keep_ref[zo] = kept_ref[zo * 2 + xh] + got_ref[zo * 2 + xh]
        send_ref[zo] = kept_ref[zo * 2 + 1 - xh] + got_ref[zo * 2 + 1 - xh]


def cross_kernel(partner_ref, high_ref, low_ref, mate_ref, out_ref, rows_ref):
    me = member()
    offset = partner_ref[pl.ds(lax.axis_index("grp"), 1), :][0, 1]
    shift = offset // BAND
    row = lax.broadcasted_iota(jnp.int32, (RUN, FEATS), 0) + lax.rem(offset, BAND)

    for i in range(QUAD):
        source = me ^ NEAR[i]
        for band in range(BANDS):
            low = ((lax.rem(band + shift, BANDS) ^ FIRST) * QUAD + source) ^ SECOND
            high = ((lax.rem(band + shift + 1, BANDS) ^ FIRST) * QUAD + source) ^ SECOND
            for xh in range(2):
                rows_ref[pl.ds((band * 2 + xh) * RUN, RUN), columns(i)] = jnp.where(
                    row + run_of(me, xh) * RUN >= BAND, mate_ref[high, xh], mate_ref[low, xh]
                )

    cross = products(high_ref, low_ref, rows_ref)
    for band in range(BANDS):
        for xh in range(2):
            at = (band * 2 + xh) * RUN
            out_ref[(band % 2 * 2 + xh) ^ NARROW, band // 2] = cross[at : at + RUN]


def middle_kernel(kept_ref, got_ref, cross_ref, out_ref):
    for zo in range(4):
        out_ref[zo ^ WIDE, 0] = kept_ref[zo] + got_ref[zo]
        out_ref[zo ^ WIDE, 1] = cross_ref[0, zo] + cross_ref[1, zo] + cross_ref[2, zo] + cross_ref[3, zo]


def total_kernel(terms_ref, self_ref, cross_ref):
    total = terms_ref[0]
    for i in range(1, terms_ref.shape[0]):
        total = total + terms_ref[i]
    total = total * (1.0 / math.sqrt(K))
    self_ref[0] = total[0]
    cross_ref[0] = total[1]


def local(grads, partner):
    own = grads[0]
    chunks = exchange(own.reshape(GROUPS, BAND, FEATS), "grp", FIRST)
    above = lax.ppermute(own, "zl", SWAP)
    routed = call(route_kernel, (GROUPS * QUAD, 2, RUN, FEATS), [VMEM, VMEM], (partner, chunks), 8)
    mate = exchange(routed, ("grp", "zl", "core"), SECOND)
    near = call(stack_kernel, (2, ROWS, FEATS), [VMEM, VMEM], (own, above), 8)
    cores = lax.ppermute(near, "core", SWAP)
    scratch = [pltpu.VMEM((MINE, QUAD * FEATS), jnp.float32)]
    bands, some = (BANDS, RUN, ROWS), (4, RUN, ROWS)
    half = jax.ShapeDtypeStruct((ROWS, QUAD * FEATS), jnp.bfloat16)
    kept, sent, high, low = call(self_kernel, [bands, bands, half, half], [VMEM, VMEM], (near, cores), 12, HINT, scratch)
    kept, sent = call(half_kernel, [some] * 2, [VMEM, VMEM], (kept, lax.ppermute(sent, "zm", SWAP)), 8, 2 * HINT)
    got = lax.ppermute(sent, "xh", SWAP)
    cross = call(
        cross_kernel, (4, 4, RUN, ROWS), [VMEM] * 4, (partner, high, low, mate), 12, 0, scratch
    )
    cross = exchange(cross, ("zm", "xh"), NARROW)
    terms = call(middle_kernel, (4, 2, RUN, ROWS), [VMEM] * 3, (kept, got, cross), 8)
    terms = exchange(terms, "zo", WIDE)
    return tuple(call(total_kernel, [(1, RUN, ROWS)] * 2, [VMEM], (terms,), 8))


def solution(mesh):
    fine = Mesh(mesh.devices.reshape(GROUPS, 4, 2, 2, 2, 2), ("grp", "zo", "zm", "zl", "xh", "core"))
    feat = ("zo", "zm", "zl", "xh", "core")
    in_specs = (P("grp", None, feat), P())
    out_specs = (P("grp", feat, None), P("grp", feat, None))
    return jax.shard_map(local, mesh=fine, in_specs=in_specs, out_specs=out_specs, check_vma=False)
```

```python
import math

import jax
import jax.numpy as jnp
from jax import lax
from jax.experimental import pallas as pl
from jax.experimental.pallas import tpu as pltpu
from jax.sharding import Mesh, PartitionSpec as P

K = 16384
ROWS = 512
GROUPS = 8
FEATS = 256
QUAD = 4
BANDS = 8
BAND = 64
RUN = 8
MINE = 128
SWAP = [(0, 1), (1, 0)]
NEAR = (0, 2, 1, 3)
HINT = 5_000_000_000
FIRST, SECOND = 4, 16
NARROW, WIDE = (1, 3, 0, 2), (2, 0, 1, 3)
VMEM = pl.BlockSpec(memory_space=pltpu.VMEM)


def exchange(values, axes, first):
    members = [i ^ first for i in range(values.shape[0])]
    return lax.all_to_all(values, axes, 0, 0, axis_index_groups=[members])


def call(kernel, shape, specs, arrays, limit, flops=0, scratch=()):
    def one(dims):
        return dims if isinstance(dims, jax.ShapeDtypeStruct) else jax.ShapeDtypeStruct(dims, jnp.float32)

    several = isinstance(shape, list)
    return pl.pallas_call(
        kernel,
        out_shape=[one(dims) for dims in shape] if several else one(shape),
        in_specs=specs,
        out_specs=[VMEM] * len(shape) if several else VMEM,
        scratch_shapes=scratch,
        compiler_params=pltpu.CompilerParams(vmem_limit_bytes=limit << 20),
        cost_estimate=pl.CostEstimate(flops=flops, bytes_accessed=0, transcendentals=0),
        name=kernel.__name__,
    )(*arrays)


def run_of(member, xh):
    return member // 2 * 4 + xh * 2 + lax.rem(member, 2)


def route_kernel(partner_ref, rows_ref, out_ref):
    partner = partner_ref[...]
    for g in range(GROUPS):
        turn = lax.rem(BAND - lax.rem(partner[g, 1], BAND), BAND)
        band = pltpu.roll(rows_ref[partner[g, 0] ^ FIRST], turn, 0)
        for m in range(QUAD):
            for xh in range(2):
                at = (m // 2 * 4 + xh * 2 + m % 2) * RUN
                out_ref[(g * QUAD + m) ^ SECOND, xh] = band[at : at + RUN]


def stack_kernel(own_ref, above_ref, near_ref):
    near_ref[0] = own_ref[...]
    near_ref[1] = above_ref[...]


def halves(values):
    high = values.astype(jnp.bfloat16)
    return high, (values - high.astype(jnp.float32)).astype(jnp.bfloat16)


def dot(left, right):
    return lax.dot_general(left, right, (((1,), (1,)), ((), ())), preferred_element_type=jnp.float32)


def products(high_ref, low_ref, rows_ref):
    rows_high, rows_low = halves(rows_ref[...])
    part = dot(high_ref[...], jnp.concatenate([rows_high, rows_low], axis=0))
    return (part[:, :MINE] + part[:, MINE:] + dot(low_ref[...], rows_high)).T


def columns(i):
    return pl.ds(i * FEATS, FEATS)


def blocks_of(near_ref, cores_ref):
    return [near_ref.at[0], near_ref.at[1], cores_ref.at[0], cores_ref.at[1]]


def member():
    return lax.axis_index("zl") * 2 + lax.axis_index("core")


def self_kernel(near_ref, cores_ref, keep_ref, send_ref, high_ref, low_ref, rows_ref):
    me = member()
    zm = lax.axis_index("zm")
    blocks = blocks_of(near_ref, cores_ref)

    for i in range(QUAD):
        high_ref[:, columns(i)], low_ref[:, columns(i)] = halves(blocks[i][...])
        for part in range(2):
            for at in range(BANDS):
                band = at // 2 * 2 + (zm ^ part)
                start = pl.multiple_of(band * BAND + run_of(me, at % 2) * RUN, RUN)
                rows_ref[pl.ds((part * BANDS + at) * RUN, RUN), columns(i)] = blocks[i][pl.ds(start, RUN), :]

    result = products(high_ref, low_ref, rows_ref)
    for band in range(BANDS):
        keep_ref[band] = result[band * RUN : (band + 1) * RUN]
        send_ref[band] = result[(BANDS + band) * RUN : (BANDS + band + 1) * RUN]


def half_kernel(kept_ref, got_ref, keep_ref, send_ref):
    xh = lax.axis_index("xh")
    for zo in range(4):
        keep_ref[zo] = kept_ref[zo * 2 + xh] + got_ref[zo * 2 + xh]
        send_ref[zo] = kept_ref[zo * 2 + 1 - xh] + got_ref[zo * 2 + 1 - xh]


def cross_kernel(partner_ref, high_ref, low_ref, mate_ref, out_ref, rows_ref):
    me = member()
    offset = partner_ref[pl.ds(lax.axis_index("grp"), 1), :][0, 1]
    shift = offset // BAND
    row = lax.broadcasted_iota(jnp.int32, (RUN, FEATS), 0) + lax.rem(offset, BAND)

    for i in range(QUAD):
        source = me ^ NEAR[i]
        for band in range(BANDS):
            low = ((lax.rem(band + shift, BANDS) ^ FIRST) * QUAD + source) ^ SECOND
            high = ((lax.rem(band + shift + 1, BANDS) ^ FIRST) * QUAD + source) ^ SECOND
            for xh in range(2):
                rows_ref[pl.ds((band * 2 + xh) * RUN, RUN), columns(i)] = jnp.where(
                    row + run_of(me, xh) * RUN >= BAND, mate_ref[high, xh], mate_ref[low, xh]
                )

    cross = products(high_ref, low_ref, rows_ref)
    for band in range(BANDS):
        for xh in range(2):
            at = (band * 2 + xh) * RUN
            out_ref[NARROW.index(band % 2 * 2 + xh), band // 2] = cross[at : at + RUN]


def middle_kernel(kept_ref, got_ref, cross_ref, out_ref):
    for zo in range(4):
        out_ref[WIDE.index(zo), 0] = kept_ref[zo] + got_ref[zo]
        out_ref[WIDE.index(zo), 1] = cross_ref[0, zo] + cross_ref[1, zo] + cross_ref[2, zo] + cross_ref[3, zo]


def total_kernel(terms_ref, self_ref, cross_ref):
    total = terms_ref[0]
    for i in range(1, terms_ref.shape[0]):
        total = total + terms_ref[i]
    total = total * (1.0 / math.sqrt(K))
    self_ref[0] = total[0]
    cross_ref[0] = total[1]


def local(grads, partner):
    own = grads[0]
    chunks = exchange(own.reshape(GROUPS, BAND, FEATS), "grp", FIRST)
    above = lax.ppermute(own, "zl", SWAP)
    routed = call(route_kernel, (GROUPS * QUAD, 2, RUN, FEATS), [VMEM, VMEM], (partner, chunks), 8)
    mate = exchange(routed, ("grp", "zl", "core"), SECOND)
    near = call(stack_kernel, (2, ROWS, FEATS), [VMEM, VMEM], (own, above), 8)
    cores = lax.ppermute(near, "core", SWAP)
    scratch = [pltpu.VMEM((MINE, QUAD * FEATS), jnp.float32)]
    bands, some = (BANDS, RUN, ROWS), (4, RUN, ROWS)
    half = jax.ShapeDtypeStruct((ROWS, QUAD * FEATS), jnp.bfloat16)
    kept, sent, high, low = call(self_kernel, [bands, bands, half, half], [VMEM, VMEM], (near, cores), 12, HINT, scratch)
    kept, sent = call(half_kernel, [some] * 2, [VMEM, VMEM], (kept, lax.ppermute(sent, "zm", SWAP)), 8, 2 * HINT)
    got = lax.ppermute(sent, "xh", SWAP)
    cross = call(
        cross_kernel, (4, 4, RUN, ROWS), [VMEM] * 4, (partner, high, low, mate), 12, 0, scratch
    )
    cross = lax.all_to_all(cross, ("zm", "xh"), 0, 0, axis_index_groups=[list(NARROW)])
    terms = call(middle_kernel, (4, 2, RUN, ROWS), [VMEM] * 3, (kept, got, cross), 8)
    terms = lax.all_to_all(terms, "zo", 0, 0, axis_index_groups=[list(WIDE)])
    return tuple(call(total_kernel, [(1, RUN, ROWS)] * 2, [VMEM], (terms,), 8))


def solution(mesh):
    fine = Mesh(mesh.devices.reshape(GROUPS, 4, 2, 2, 2, 2), ("grp", "zo", "zm", "zl", "xh", "core"))
    feat = ("zo", "zm", "zl", "xh", "core")
    in_specs = (P("grp", None, feat), P())
    out_specs = (P("grp", feat, None), P("grp", feat, None))
    return jax.shard_map(local, mesh=fine, in_specs=in_specs, out_specs=out_specs, check_vma=False)
```

```python
import math

import jax
import jax.numpy as jnp
from jax import lax
from jax.experimental import pallas as pl
from jax.experimental.pallas import tpu as pltpu
from jax.sharding import Mesh, PartitionSpec as P

K = 16384
ROWS = 512
GROUPS = 8
FEATS = 256
QUAD = 4
BANDS = 8
BAND = 64
RUN = 8
MINE = 128
SWAP = [(0, 1), (1, 0)]
NEAR = (0, 2, 1, 3)
HINT = 5_000_000_000
FIRST, SECOND, NARROW, WIDE = 6, 24, 1, 2
VMEM = pl.BlockSpec(memory_space=pltpu.VMEM)


def exchange(values, axes, first):
    members = [i ^ first for i in range(values.shape[0])]
    return lax.all_to_all(values, axes, 0, 0, axis_index_groups=[members])


def call(kernel, shape, specs, arrays, limit, flops=0, scratch=()):
    def one(dims):
        return dims if isinstance(dims, jax.ShapeDtypeStruct) else jax.ShapeDtypeStruct(dims, jnp.float32)

    several = isinstance(shape, list)
    return pl.pallas_call(
        kernel,
        out_shape=[one(dims) for dims in shape] if several else one(shape),
        in_specs=specs,
        out_specs=[VMEM] * len(shape) if several else VMEM,
        scratch_shapes=scratch,
        compiler_params=pltpu.CompilerParams(vmem_limit_bytes=limit << 20),
        cost_estimate=pl.CostEstimate(flops=flops, bytes_accessed=0, transcendentals=0),
        name=kernel.__name__,
    )(*arrays)


def run_of(member, xh):
    return member // 2 * 4 + xh * 2 + lax.rem(member, 2)


def route_kernel(partner_ref, rows_ref, out_ref):
    partner = partner_ref[...]
    for g in range(GROUPS):
        turn = lax.rem(BAND - lax.rem(partner[g, 1], BAND), BAND)
        band = pltpu.roll(rows_ref[partner[g, 0] ^ FIRST], turn, 0)
        for m in range(QUAD):
            for xh in range(2):
                at = (m // 2 * 4 + xh * 2 + m % 2) * RUN
                out_ref[(g * QUAD + m) ^ SECOND, xh] = band[at : at + RUN]


def stack_kernel(own_ref, above_ref, near_ref):
    near_ref[0] = own_ref[...]
    near_ref[1] = above_ref[...]


def halves(values):
    high = values.astype(jnp.bfloat16)
    return high, (values - high.astype(jnp.float32)).astype(jnp.bfloat16)


def dot(left, right):
    return lax.dot_general(left, right, (((1,), (1,)), ((), ())), preferred_element_type=jnp.float32)


def products(high_ref, low_ref, rows_ref):
    rows_high, rows_low = halves(rows_ref[...])
    part = dot(high_ref[...], jnp.concatenate([rows_high, rows_low], axis=0))
    return (part[:, :MINE] + part[:, MINE:] + dot(low_ref[...], rows_high)).T


def columns(i):
    return pl.ds(i * FEATS, FEATS)


def blocks_of(near_ref, cores_ref):
    return [near_ref.at[0], near_ref.at[1], cores_ref.at[0], cores_ref.at[1]]


def member():
    return lax.axis_index("zl") * 2 + lax.axis_index("core")


def self_kernel(near_ref, cores_ref, keep_ref, send_ref, high_ref, low_ref, rows_ref):
    me = member()
    zm = lax.axis_index("zm")
    blocks = blocks_of(near_ref, cores_ref)

    for i in range(QUAD):
        high_ref[:, columns(i)], low_ref[:, columns(i)] = halves(blocks[i][...])
        for part in range(2):
            for at in range(BANDS):
                band = at // 2 * 2 + (zm ^ part)
                start = pl.multiple_of(band * BAND + run_of(me, at % 2) * RUN, RUN)
                rows_ref[pl.ds((part * BANDS + at) * RUN, RUN), columns(i)] = blocks[i][pl.ds(start, RUN), :]

    result = products(high_ref, low_ref, rows_ref)
    for band in range(BANDS):
        keep_ref[band] = result[band * RUN : (band + 1) * RUN]
        send_ref[band] = result[(BANDS + band) * RUN : (BANDS + band + 1) * RUN]


def half_kernel(kept_ref, got_ref, keep_ref, send_ref):
    xh = lax.axis_index("xh")
    for zo in range(4):
        keep_ref[zo] = kept_ref[zo * 2 + xh] + got_ref[zo * 2 + xh]
        send_ref[zo] = kept_ref[zo * 2 + 1 - xh] + got_ref[zo * 2 + 1 - xh]


def cross_kernel(partner_ref, high_ref, low_ref, mate_ref, out_ref, rows_ref):
    me = member()
    offset = partner_ref[pl.ds(lax.axis_index("grp"), 1), :][0, 1]
    shift = offset // BAND
    row = lax.broadcasted_iota(jnp.int32, (RUN, FEATS), 0) + lax.rem(offset, BAND)

    for i in range(QUAD):
        source = me ^ NEAR[i]
        for band in range(BANDS):
            low = ((lax.rem(band + shift, BANDS) ^ FIRST) * QUAD + source) ^ SECOND
            high = ((lax.rem(band + shift + 1, BANDS) ^ FIRST) * QUAD + source) ^ SECOND
            for xh in range(2):
                rows_ref[pl.ds((band * 2 + xh) * RUN, RUN), columns(i)] = jnp.where(
                    row + run_of(me, xh) * RUN >= BAND, mate_ref[high, xh], mate_ref[low, xh]
                )

    cross = products(high_ref, low_ref, rows_ref)
    for band in range(BANDS):
        for xh in range(2):
            at = (band * 2 + xh) * RUN
            out_ref[(band % 2 * 2 + xh) ^ NARROW, band // 2] = cross[at : at + RUN]


def middle_kernel(kept_ref, got_ref, cross_ref, out_ref):
    for zo in range(4):
        out_ref[zo ^ WIDE, 0] = kept_ref[zo] + got_ref[zo]
        out_ref[zo ^ WIDE, 1] = cross_ref[0, zo] + cross_ref[1, zo] + cross_ref[2, zo] + cross_ref[3, zo]


def total_kernel(terms_ref, self_ref, cross_ref):
    total = terms_ref[0]
    for i in range(1, terms_ref.shape[0]):
        total = total + terms_ref[i]
    total = total * (1.0 / math.sqrt(K))
    self_ref[0] = total[0]
    cross_ref[0] = total[1]


def local(grads, partner):
    own = grads[0]
    chunks = exchange(own.reshape(GROUPS, BAND, FEATS), "grp", FIRST)
    above = lax.ppermute(own, "zl", SWAP)
    routed = call(route_kernel, (GROUPS * QUAD, 2, RUN, FEATS), [VMEM, VMEM], (partner, chunks), 8)
    mate = exchange(routed, ("grp", "zl", "core"), SECOND)
    near = call(stack_kernel, (2, ROWS, FEATS), [VMEM, VMEM], (own, above), 8)
    cores = lax.ppermute(near, "core", SWAP)
    scratch = [pltpu.VMEM((MINE, QUAD * FEATS), jnp.float32)]
    bands, some = (BANDS, RUN, ROWS), (4, RUN, ROWS)
    half = jax.ShapeDtypeStruct((ROWS, QUAD * FEATS), jnp.bfloat16)
    kept, sent, high, low = call(self_kernel, [bands, bands, half, half], [VMEM, VMEM], (near, cores), 12, HINT, scratch)
    kept, sent = call(half_kernel, [some] * 2, [VMEM, VMEM], (kept, lax.ppermute(sent, "zm", SWAP)), 8, 2 * HINT)
    got = lax.ppermute(sent, "xh", SWAP)
    cross = call(
        cross_kernel, (4, 4, RUN, ROWS), [VMEM] * 4, (partner, high, low, mate), 12, 0, scratch
    )
    cross = exchange(cross, ("zm", "xh"), NARROW)
    terms = call(middle_kernel, (4, 2, RUN, ROWS), [VMEM] * 3, (kept, got, cross), 8)
    terms = exchange(terms, "zo", WIDE)
    return tuple(call(total_kernel, [(1, RUN, ROWS)] * 2, [VMEM], (terms,), 8))


def solution(mesh):
    fine = Mesh(mesh.devices.reshape(GROUPS, 4, 2, 2, 2, 2), ("grp", "zo", "zm", "zl", "xh", "core"))
    feat = ("zo", "zm", "zl", "xh", "core")
    in_specs = (P("grp", None, feat), P())
    out_specs = (P("grp", feat, None), P("grp", feat, None))
    return jax.shard_map(local, mesh=fine, in_specs=in_specs, out_specs=out_specs, check_vma=False)
```
